1024 devices in a mesh: outer: 128 (over y, z_lo, x), inner: 8 (over z_hi, core).
Axes of the slice: x: 8, y: 8, z: 8 (z_hi: 4, z_lo: 2; z = z_hi * 2 + z_lo), core: 2. Of those that a mesh axis runs over, the one named last changes fastest.
Arguments:
- photo_embedding_matrix: bfloat16 [131072, 1152], P(('outer', 'inner')), may hold values from -1 to 1
- sentence_embedding_matrix: bfloat16 [131072, 1152], P(('outer', 'inner')), may hold values from -1 to 1
- logit_stretch_factor: float32 [1], replicated, may hold values from 4 to 8
- logit_offset_term: float32 [1], replicated, may hold values from -4 to -2
Outputs:
- grad_image: float32 [131072, 1152], P(('outer', 'inner'))
- grad_text: float32 [131072, 1152], P(('outer', 'inner'))
The draws below stay inside these ranges and needn't reach their ends.
All inputs are finite; a program needn't handle non-finite values.
Results may differ from the reference program's by a relative error of at most 0.0027.
Values may be sent and summed in bfloat16 or wider, within the bound.
No kernel may reach another device: no remote copies, remote signals or barrier semaphores. Data moves between devices by JAX's collectives and lax.ppermute only.
A program may use at most 32 MiB of HBM per device.

```python
import jax
import jax.numpy as jnp
from jax import lax

D = 1152
ROWS = 128
BATCH = 131072
N_OUTER = 128
N_INNER = 8


def shared_base(key):
    return jax.random.normal(jax.random.fold_in(key, 11), (BATCH, D), jnp.float32) * D ** (-0.5)


def draw_photo_embedding_matrix(key, part):
    base = shared_base(key)
    return jnp.clip(base, -1.0, 1.0).astype(jnp.bfloat16)


def draw_sentence_embedding_matrix(key, part):
    base = shared_base(key)
    key = jax.random.fold_in(key, 7)
    mixing = jax.random.uniform(jax.random.fold_in(key, 1), (BATCH, 1), jnp.float32, 0.0, 0.9)
    noise = jax.random.normal(jax.random.fold_in(key, 2), (BATCH, D), jnp.float32) * D ** (-0.5)
    return jnp.clip(mixing * base + jnp.sqrt(1.0 - mixing * mixing) * noise, -1.0, 1.0).astype(jnp.bfloat16)


def setup_inputs(seed: int = 0) -> dict:
    streams_of = jax.random.split(jax.random.key(seed), 5)
    return {
        "photo_embedding_matrix": draw_photo_embedding_matrix(jax.random.fold_in(streams_of[4], 71), 0),
        "sentence_embedding_matrix": draw_sentence_embedding_matrix(jax.random.fold_in(streams_of[4], 71), 0),
        "logit_stretch_factor": jnp.clip(jax.random.uniform(streams_of[2], (1,), jnp.float32, 4.0, 8.0), 4.0, 8.0),
        "logit_offset_term": jnp.clip(jax.random.uniform(streams_of[3], (1,), jnp.float32, -4.0, -2.0), -4.0, -2.0),
    }


def signed_multiplier(left_rows, right_rows, reciprocal_logit_temp, offset, positive):
    scores = reciprocal_logit_temp * lax.dot_general(left_rows, right_rows, (((1,), (1,)), ((), ())), preferred_element_type=jnp.float32) + offset
    signs = jnp.where(positive, 1.0, -1.0).astype(jnp.float32)
    return (-signs * jax.nn.sigmoid(-signs * scores) * reciprocal_logit_temp).astype(jnp.bfloat16)


def reference(photo_embedding_matrix, sentence_embedding_matrix, logit_stretch_factor, logit_offset_term):
    block_rows = ROWS * N_INNER
    reciprocal_logit_temp = logit_stretch_factor[0]
    offset = logit_offset_term[0]
    local_picture_rows = photo_embedding_matrix.reshape(N_OUTER, block_rows, D)
    next_images = jnp.roll(local_picture_rows, -1, axis=0)
    group_text = sentence_embedding_matrix.reshape(N_OUTER, block_rows, D)
    row_index = lax.broadcasted_iota(jnp.int32, (block_rows, block_rows), 0)
    column_position = lax.broadcasted_iota(jnp.int32, (block_rows, block_rows), 1)
    positive = row_index == column_position
    nothing = row_index < 0

    def per_group(items):
        mine, visiting_partner_blocks, texts = items
        own_coef = signed_multiplier(mine, texts, reciprocal_logit_temp, offset, positive)
        guest_coef = signed_multiplier(visiting_partner_blocks, texts, reciprocal_logit_temp, offset, nothing)
        own_grad = jnp.dot(own_coef, texts, preferred_element_type=jnp.float32)
        guest_grad = jnp.dot(guest_coef, texts, preferred_element_type=jnp.float32)
        sentence_slice_share = jnp.dot(own_coef.T, mine, preferred_element_type=jnp.float32)
        sentence_slice_share = sentence_slice_share + jnp.dot(guest_coef.T, visiting_partner_blocks, preferred_element_type=jnp.float32)
        return own_grad, guest_grad, sentence_slice_share

    own_grad, guest_grad, sentence_slice_share = lax.map(per_group, (local_picture_rows, next_images, group_text))
    grad_image = own_grad + jnp.roll(guest_grad, 1, axis=0)
    return grad_image.reshape(BATCH, D), sentence_slice_share.reshape(BATCH, D)
```

```python
import jax
import jax.numpy as jnp
from jax import lax
from jax.sharding import PartitionSpec as P

F32 = jnp.float32
BF16 = jnp.bfloat16


def inner_route(move, devices):
    route = []
    for chip in range(devices // 2):
        for core in range(2):
            to_chip, to_core = move(chip, core)
            route.append((chip * 2 + core, to_chip * 2 + to_core))
    return route


def per_device(images, texts, stretch, offset_term):
    outer, inner = lax.axis_size("outer"), lax.axis_size("inner")
    chips = inner // 2
    rows = images.shape[0]
    scale, offset = stretch[0], offset_term[0]

    across = inner_route(lambda z, c: (chips - 1 - z, c), inner)
    beside = inner_route(lambda z, c: (z ^ 1, c), inner)
    other_core = inner_route(lambda z, c: (z, 1 - c), inner)
    to_previous = [(i, (i - 1) % outer) for i in range(outer)]
    to_next = [(i, (i + 1) % outer) for i in range(outer)]

    images_across = lax.ppermute(images, "inner", across)
    guests = lax.ppermute(images, "outer", to_previous)
    texts_beside = lax.ppermute(texts, "inner", beside)
    texts_core = lax.ppermute(texts, "inner", other_core)
    texts_beside_core = lax.ppermute(texts_beside, "inner", other_core)
    guests_across = lax.ppermute(images_across, "outer", to_previous)
    all_texts = jnp.concatenate([texts, texts_beside, texts_core, texts_beside_core], axis=0)

    row = lax.broadcasted_iota(jnp.int32, (rows, 4 * rows), 0)
    column = lax.broadcasted_iota(jnp.int32, (rows, 4 * rows), 1)

    def coefficients(left, positive):
        scores = scale * lax.dot_general(
            left, all_texts, (((1,), (1,)), ((), ())), preferred_element_type=F32
        ) + offset
        signs = jnp.where(positive, 1.0, -1.0).astype(F32)
        return (-signs * jax.nn.sigmoid(-signs * scores) * scale).astype(BF16)

    def image_part(coef):
        return jnp.dot(coef, all_texts, preferred_element_type=F32)

    def text_part(coef, left):
        return lax.dot_general(coef, left, (((0,), (0,)), ((), ())), preferred_element_type=F32)

    nothing = column < 0
    coef = coefficients(images, row == column)
    coef_across = coefficients(images_across, nothing)
    coef_guests = coefficients(guests, nothing)
    coef_guests_across = coefficients(guests_across, nothing)

    back_across = lax.ppermute(image_part(coef_guests_across).astype(BF16), "outer", to_next)
    back = lax.ppermute(image_part(coef_guests).astype(BF16), "outer", to_next)
    own = image_part(coef)
    own_across = image_part(coef_across)

    grad_texts = (
        text_part(coef, images)
        + text_part(coef_across, images_across)
        + text_part(coef_guests, guests)
        + text_part(coef_guests_across, guests_across)
    )
    mine, beside_mine, core, beside_core = (
        grad_texts[k * rows : (k + 1) * rows] for k in range(4)
    )
    beside_from_core = lax.ppermute(beside_core.astype(BF16), "inner", other_core)
    from_core = lax.ppermute(core.astype(BF16), "inner", other_core)
    from_beside = lax.ppermute(
        (beside_mine + beside_from_core.astype(F32)).astype(BF16), "inner", beside
    )
    from_across = lax.ppermute(
        (own_across + back_across.astype(F32)).astype(BF16), "inner", across
    )
    grad_image = own + back.astype(F32) + from_across.astype(F32)
    grad_text = mine + from_core.astype(F32) + from_beside.astype(F32)
    return grad_image, grad_text


def solution(mesh):
    block = P(("outer", "inner"), None)
    return jax.shard_map(
        per_device,
        mesh=mesh,
        in_specs=(block, block, P(), P()),
        out_specs=(block, block),
        check_vma=False,
    )
```

```python
import jax
import jax.numpy as jnp
from jax import lax
from jax.sharding import PartitionSpec as P

F32 = jnp.float32
BF16 = jnp.bfloat16


def inner_route(move, devices):
    route = []
    for chip in range(devices // 2):
        for core in range(2):
            to_chip, to_core = move(chip, core)
            route.append((chip * 2 + core, to_chip * 2 + to_core))
    return route


def per_device(images, texts, stretch, offset_term):
    outer, inner = lax.axis_size("outer"), lax.axis_size("inner")
    chips = inner // 2
    rows = images.shape[0]
    scale, offset = stretch[0], offset_term[0]

    across = inner_route(lambda z, c: (chips - 1 - z, c), inner)
    beside = inner_route(lambda z, c: (z ^ 1, c), inner)
    other_core = inner_route(lambda z, c: (z, 1 - c), inner)
    to_previous = [(i, (i - 1) % outer) for i in range(outer)]
    to_next = [(i, (i + 1) % outer) for i in range(outer)]

    images_across = lax.ppermute(images, "inner", across)
    texts_beside = lax.ppermute(texts, "inner", beside)
    texts_core = lax.ppermute(texts, "inner", other_core)
    guests = lax.ppermute(images, "outer", to_previous)
    guests_across = lax.ppermute(images_across, "outer", to_previous)
    texts_beside_core = lax.ppermute(texts_beside, "inner", other_core)
    all_texts = jnp.concatenate([texts, texts_beside, texts_core, texts_beside_core], axis=0)

    row = lax.broadcasted_iota(jnp.int32, (rows, 4 * rows), 0)
    column = lax.broadcasted_iota(jnp.int32, (rows, 4 * rows), 1)

    def coefficients(left, positive):
        scores = scale * lax.dot_general(
            left, all_texts, (((1,), (1,)), ((), ())), preferred_element_type=F32
        ) + offset
        signs = jnp.where(positive, 1.0, -1.0).astype(F32)
        return (-signs * jax.nn.sigmoid(-signs * scores) * scale).astype(BF16)

    def image_part(coef):
        return jnp.dot(coef, all_texts, preferred_element_type=F32)

    def text_part(coef, left):
        return lax.dot_general(coef, left, (((0,), (0,)), ((), ())), preferred_element_type=F32)

    nothing = column < 0
    coef_guests = coefficients(guests, nothing)
    guests_part = image_part(coef_guests).astype(BF16)
    back = lax.ppermute(guests_part, "outer", to_next)

    coef_guests_across = coefficients(guests_across, nothing)
    guests_across_part = image_part(coef_guests_across).astype(BF16)
    back_across = lax.ppermute(guests_across_part, "outer", to_next)

    coef = coefficients(images, row == column)
    coef_across = coefficients(images_across, nothing)
    grad_texts = (
        text_part(coef, images)
        + text_part(coef_across, images_across)
        + text_part(coef_guests, guests)
        + text_part(coef_guests_across, guests_across)
    )
    from_core = lax.ppermute(grad_texts[2 * rows :].astype(BF16), "inner", other_core)
    own = image_part(coef)
    own_across = image_part(coef_across)
    both = grad_texts[: 2 * rows] + from_core.astype(F32)
    own, own_across, back_across = lax.optimization_barrier((own, own_across, back_across))
    from_beside = lax.ppermute(both[rows:].astype(BF16), "inner", beside)
    from_across = lax.ppermute(
        (own_across + back_across.astype(F32)).astype(BF16), "inner", across
    )
    grad_text = both[:rows] + from_beside.astype(F32)
    grad_image = own + back.astype(F32) + from_across.astype(F32)
    return grad_image, grad_text


def solution(mesh):
    block = P(("outer", "inner"), None)
    return jax.shard_map(
        per_device,
        mesh=mesh,
        in_specs=(block, block, P(), P()),
        out_specs=(block, block),
        check_vma=False,
    )
```

```python
import jax
import jax.numpy as jnp
from jax import lax
from jax.experimental import pallas as pl
from jax.experimental.pallas import tpu as pltpu
from jax.sharding import PartitionSpec as P

F32 = jnp.float32
BF16 = jnp.bfloat16
BY_COLUMN = (((0,), (0,)), ((), ()))
BY_ROW = (((1,), (1,)), ((), ()))


def inner_route(move, devices):
    route = []
    for chip in range(devices // 2):
        for core in range(2):
            to_chip, to_core = move(chip, core)
            route.append((chip * 2 + core, to_chip * 2 + to_core))
    return route


def coefficients(left, right, scale, offset, has_diagonal=False):
    scores = scale * lax.dot_general(left, right, BY_ROW, preferred_element_type=F32) + offset
    coef = scale * jax.nn.sigmoid(scores)
    if has_diagonal:
        shape = scores.shape
        same = lax.broadcasted_iota(jnp.int32, shape, 0) == lax.broadcasted_iota(jnp.int32, shape, 1)
        coef = jnp.where(same, -scale * jax.nn.sigmoid(-scores), coef)
    return coef.astype(BF16)


def last_guests_kernel(stretch, offset_term, left, t0, t1, t2, t3, coef, part):
    scale, offset = stretch[0], offset_term[0]
    rows = left.shape[0]
    total = None
    for k, text in enumerate((t0, t1, t2, t3)):
        c = coefficients(left[...], text[...], scale, offset)
        coef[:, k * rows : (k + 1) * rows] = c
        term = jnp.dot(c, text[...], preferred_element_type=F32)
        total = term if total is None else total + term
    part[...] = total.astype(BF16)


def rest_kernel(
    stretch, offset_term, images, across, guests, last, last_coef, t0, t1, t2, t3,
    own, own_across, guests_part, mine, far, for_core,
):
    scale, offset = stretch[0], offset_term[0]
    rows = images.shape[0]
    sums = [None, None, None]
    lefts = (images[...], across[...], guests[...])
    for k, text in enumerate((t0, t1, t2, t3)):
        right = text[...]
        grad = lax.dot_general(
            last_coef[:, k * rows : (k + 1) * rows], last[...], BY_COLUMN, preferred_element_type=F32
        )
        for i, left in enumerate(lefts):
            c = coefficients(left, right, scale, offset, has_diagonal=(i == 0 and k == 0))
            term = jnp.dot(c, right, preferred_element_type=F32)
            sums[i] = term if sums[i] is None else sums[i] + term
            grad = grad + lax.dot_general(c, left, BY_COLUMN, preferred_element_type=F32)
        if k == 0:
            mine[...] = grad
        elif k == 1:
            for_core[rows:, :] = grad.astype(BF16)
        elif k == 2:
            far[...] = grad
        else:
            for_core[:rows, :] = grad.astype(BF16)
    own[...] = sums[0]
    own_across[...] = sums[1]
    guests_part[...] = sums[2].astype(BF16)


def local_call(kernel, outs, flops, stretch, offset_term, *arrays):
    vmem = pl.BlockSpec(memory_space=pltpu.VMEM)
    return pl.pallas_call(
        kernel,
        out_shape=[jax.ShapeDtypeStruct(shape, dtype) for shape, dtype in outs],
        in_specs=[pl.BlockSpec(memory_space=pltpu.SMEM)] * 2 + [vmem] * len(arrays),
        out_specs=[vmem] * len(outs),
        compiler_params=pltpu.CompilerParams(vmem_limit_bytes=24 * 1024 * 1024),
        cost_estimate=pl.CostEstimate(flops=flops, bytes_accessed=0, transcendentals=0),
    )(stretch, offset_term, *arrays)


def per_device(images, texts, stretch, offset_term):
    outer, inner = lax.axis_size("outer"), lax.axis_size("inner")
    chips = inner // 2
    rows, width = images.shape

    across = inner_route(lambda z, c: (chips - 1 - z, c), inner)
    beside = inner_route(lambda z, c: (z ^ 1, c), inner)
    other_core = inner_route(lambda z, c: (z, 1 - c), inner)
    to_previous = [(i, (i - 1) % outer) for i in range(outer)]
    to_next = [(i, (i + 1) % outer) for i in range(outer)]

    images_across = lax.ppermute(images, "inner", across)
    texts_core = lax.ppermute(texts, "inner", other_core)
    texts_beside = lax.ppermute(texts, "inner", beside)
    guests = lax.ppermute(images, "outer", to_previous)
    guests_across = lax.ppermute(images_across, "outer", to_previous)
    texts_beside_core = lax.ppermute(texts_beside, "inner", other_core)
    all_texts = (texts, texts_core, texts_beside, texts_beside_core)

    block = rows * width * 4 * rows * 2
    last_coef, last_part = local_call(
        last_guests_kernel,
        [((rows, 4 * rows), BF16), ((rows, width), BF16)],
        2 * block,
        stretch, offset_term, guests_across, *all_texts,
    )
    back_across = lax.ppermute(last_part, "outer", to_next)
    own, own_across, guests_part, mine, far, for_core = local_call(
        rest_kernel,
        [
            ((rows, width), F32), ((rows, width), F32), ((rows, width), BF16),
            ((rows, width), F32), ((rows, width), F32), ((2 * rows, width), BF16),
        ],
        10 * block,
        stretch, offset_term, images, images_across, guests, guests_across, last_coef, *all_texts,
    )
    from_core = lax.ppermute(for_core, "inner", other_core)
    back = lax.ppermute(guests_part, "outer", to_next)
    own, own_across, back_across = lax.optimization_barrier((own, own_across, back_across))
    mine = mine + from_core[rows:].astype(F32)
    sent = (far + from_core[:rows].astype(F32)).astype(BF16)
    from_beside = lax.ppermute(sent, "inner", beside)
    from_across = lax.ppermute(
        (own_across + back_across.astype(F32)).astype(BF16), "inner", across
    )
    grad_text = mine + from_beside.astype(F32)
    grad_image = own + back.astype(F32) + from_across.astype(F32)
    return grad_image, grad_text


def solution(mesh):
    block = P(("outer", "inner"), None)
    return jax.shard_map(
        per_device,
        mesh=mesh,
        in_specs=(block, block, P(), P()),
        out_specs=(block, block),
        check_vma=False,
    )
```

```python
import jax
import jax.numpy as jnp
from jax import lax
from jax.experimental import pallas as pl
from jax.experimental.pallas import tpu as pltpu
from jax.sharding import PartitionSpec as P

F32 = jnp.float32
BF16 = jnp.bfloat16
BY_COLUMN = (((0,), (0,)), ((), ()))
BY_ROW = (((1,), (1,)), ((), ()))


def inner_route(move, devices):
    route = []
    for chip in range(devices // 2):
        for core in range(2):
            to_chip, to_core = move(chip, core)
            route.append((chip * 2 + core, to_chip * 2 + to_core))
    return route


def stack(*refs):
    return jnp.concatenate([ref[...] for ref in refs], axis=0)


def scores_of(left, right, stretch, offset_term):
    product = lax.dot_general(left, right, BY_ROW, preferred_element_type=F32)
    return stretch[0] * product + offset_term[0]


def guests_kernel(stretch, offset_term, left, t0, t1, t2, t3, coef, part):
    texts = stack(t0, t1, t2, t3)
    scores = scores_of(left[...], texts, stretch, offset_term)
    c = (stretch[0] * jax.nn.sigmoid(scores)).astype(BF16)
    coef[...] = c
    part[...] = jnp.dot(c, texts, preferred_element_type=F32).astype(BF16)


def rest_kernel(
    stretch, offset_term, images, across, guests, last, guests_coef, last_coef, t0, t1, t2, t3,
    own, own_across, mine, far, for_core,
):
    rows = images.shape[0]
    texts = stack(t0, t1, t2, t3)
    scores = scores_of(stack(images, across), texts, stretch, offset_term)
    row = lax.broadcasted_iota(jnp.int32, scores.shape, 0)
    column = lax.broadcasted_iota(jnp.int32, scores.shape, 1)
    same = (row == column) & (row < rows)
    coef = jnp.where(
        same,
        (-stretch[0] * jax.nn.sigmoid(-scores)).astype(BF16),
        (stretch[0] * jax.nn.sigmoid(scores)).astype(BF16),
    )
    image_grads = jnp.dot(coef, texts, preferred_element_type=F32)
    own[...] = image_grads[:rows]
    own_across[...] = image_grads[rows:]
    text_grads = lax.dot_general(
        jnp.concatenate([coef, guests_coef[...], last_coef[...]], axis=0),
        stack(images, across, guests, last),
        BY_COLUMN,
        preferred_element_type=F32,
    )
    mine[...] = text_grads[:rows]
    far[...] = text_grads[2 * rows : 3 * rows]
    for_core[rows:, :] = text_grads[rows : 2 * rows].astype(BF16)
    for_core[:rows, :] = text_grads[3 * rows :].astype(BF16)


def local_call(kernel, outs, flops, stretch, offset_term, *arrays):
    vmem = pl.BlockSpec(memory_space=pltpu.VMEM)
    return pl.pallas_call(
        kernel,
        out_shape=[jax.ShapeDtypeStruct(shape, dtype) for shape, dtype in outs],
        in_specs=[pl.BlockSpec(memory_space=pltpu.SMEM)] * 2 + [vmem] * len(arrays),
        out_specs=[vmem] * len(outs),
        compiler_params=pltpu.CompilerParams(vmem_limit_bytes=24 * 1024 * 1024),
        cost_estimate=pl.CostEstimate(flops=flops, bytes_accessed=0, transcendentals=0),
    )(stretch, offset_term, *arrays)


def per_device(images, texts, stretch, offset_term):
    outer, inner = lax.axis_size("outer"), lax.axis_size("inner")
    chips = inner // 2
    rows, width = images.shape

    across = inner_route(lambda z, c: (chips - 1 - z, c), inner)
    beside = inner_route(lambda z, c: (z ^ 1, c), inner)
    other_core = inner_route(lambda z, c: (z, 1 - c), inner)
    to_previous = [(i, (i - 1) % outer) for i in range(outer)]
    to_next = [(i, (i + 1) % outer) for i in range(outer)]

    images_across = lax.ppermute(images, "inner", across)
    texts_core = lax.ppermute(texts, "inner", other_core)
    texts_out = texts
    texts_beside = lax.ppermute(texts_out, "inner", beside)
    guests = lax.ppermute(images, "outer", to_previous)
    guests_across = lax.ppermute(images_across, "outer", to_previous)
    texts_beside_core = lax.ppermute(texts_beside, "inner", other_core)
    all_texts = (texts, texts_core, texts_beside, texts_beside_core)

    block = rows * width * 4 * rows * 2
    guests_outs = [((rows, 4 * rows), BF16), ((rows, width), BF16)]
    guests_coef, guests_part = local_call(
        guests_kernel, guests_outs, 2 * block, stretch, offset_term, guests, *all_texts
    )
    back = lax.ppermute(guests_part, "outer", to_next)
    last_coef, last_part = local_call(
        guests_kernel, guests_outs, 2 * block, stretch, offset_term, guests_across, *all_texts
    )
    back_across = lax.ppermute(last_part, "outer", to_next)
    own, own_across, mine, far, for_core = local_call(
        rest_kernel,
        [((rows, width), F32)] * 4 + [((2 * rows, width), BF16)],
        8 * block,
        stretch, offset_term, images, images_across, guests, guests_across,
        guests_coef, last_coef, *all_texts,
    )
    from_core = lax.ppermute(for_core, "inner", other_core)
    own = own + back.astype(F32)
    own_across, back_across = lax.optimization_barrier((own_across, back_across))
    mine = mine + from_core[rows:].astype(F32)
    sent = (far + from_core[:rows].astype(F32)).astype(BF16)
    own, sent = lax.optimization_barrier((own, sent))
    from_beside = lax.ppermute(sent, "inner", beside)
    from_across = lax.ppermute(
        (own_across + back_across.astype(F32)).astype(BF16), "inner", across
    )
    grad_text = mine + from_beside.astype(F32)
    grad_image = own + from_across.astype(F32)
    return grad_image, grad_text


def solution(mesh):
    block = P(("outer", "inner"), None)
    return jax.shard_map(
        per_device,
        mesh=mesh,
        in_specs=(block, block, P(), P()),
        out_specs=(block, block),
        check_vma=False,
    )
```

```python
import jax
import jax.numpy as jnp
from jax import lax
from jax.experimental import pallas as pl
from jax.experimental.pallas import tpu as pltpu
from jax.sharding import PartitionSpec as P

F32 = jnp.float32
BF16 = jnp.bfloat16
BY_COLUMN = (((0,), (0,)), ((), ()))
BY_ROW = (((1,), (1,)), ((), ()))


def inner_route(move, devices):
    route = []
    for chip in range(devices // 2):
        for core in range(2):
            to_chip, to_core = move(chip, core)
            route.append((chip * 2 + core, to_chip * 2 + to_core))
    return route


def stack(*refs):
    return jnp.concatenate([ref[...] for ref in refs], axis=0)


def scores_of(left, right, stretch, offset_term):
    product = lax.dot_general(left, right, BY_ROW, preferred_element_type=F32)
    return stretch[0] * product + offset_term[0]


def guests_kernel(stretch, offset_term, left, t0, t1, t2, t3, coef, part):
    texts = stack(t0, t1, t2, t3)
    scores = scores_of(left[...], texts, stretch, offset_term)
    c = (stretch[0] * jax.nn.sigmoid(scores)).astype(BF16)
    coef[...] = c
    part[...] = jnp.dot(c, texts, preferred_element_type=F32).astype(BF16)


def rest_kernel(
    stretch, offset_term, images, across, guests, last, guests_coef, last_coef, t0, t1, t2, t3,
    own, own_across, mine, far, for_core,
):
    rows = images.shape[0]
    texts = stack(t0, t1, t2, t3)
    scores = scores_of(stack(images, across), texts, stretch, offset_term)
    row = lax.broadcasted_iota(jnp.int32, scores.shape, 0)
    column = lax.broadcasted_iota(jnp.int32, scores.shape, 1)
    same = (row == column) & (row < rows)
    coef = jnp.where(
        same,
        (-stretch[0] * jax.nn.sigmoid(-scores)).astype(BF16),
        (stretch[0] * jax.nn.sigmoid(scores)).astype(BF16),
    )
    image_grads = jnp.dot(coef, texts, preferred_element_type=F32)
    own[...] = image_grads[:rows]
    own_across[...] = image_grads[rows:]
    text_grads = lax.dot_general(
        jnp.concatenate([coef, guests_coef[...], last_coef[...]], axis=0),
        stack(images, across, guests, last),
        BY_COLUMN,
        preferred_element_type=F32,
    )
    mine[...] = text_grads[:rows]
    far[...] = text_grads[2 * rows : 3 * rows]
    for_core[rows:, :] = text_grads[rows : 2 * rows].astype(BF16)
    for_core[:rows, :] = text_grads[3 * rows :].astype(BF16)


def local_call(kernel, outs, flops, stretch, offset_term, *arrays):
    vmem = pl.BlockSpec(memory_space=pltpu.VMEM)
    return pl.pallas_call(
        kernel,
        out_shape=[jax.ShapeDtypeStruct(shape, dtype) for shape, dtype in outs],
        in_specs=[pl.BlockSpec(memory_space=pltpu.SMEM)] * 2 + [vmem] * len(arrays),
        out_specs=[vmem] * len(outs),
        compiler_params=pltpu.CompilerParams(vmem_limit_bytes=24 * 1024 * 1024),
        cost_estimate=pl.CostEstimate(flops=flops, bytes_accessed=0, transcendentals=0),
    )(stretch, offset_term, *arrays)


def per_device(images, texts, stretch, offset_term):
    outer, inner = lax.axis_size("outer"), lax.axis_size("inner")
    chips = inner // 2
    rows, width = images.shape

    across = inner_route(lambda z, c: (chips - 1 - z, c), inner)
    beside = inner_route(lambda z, c: (z ^ 1, c), inner)
    other_core = inner_route(lambda z, c: (z, 1 - c), inner)
    to_previous = [(i, (i - 1) % outer) for i in range(outer)]
    to_next = [(i, (i + 1) % outer) for i in range(outer)]

    images_across = lax.ppermute(images, "inner", across)
    texts_core = lax.ppermute(texts, "inner", other_core)
    texts_out = texts
    texts_beside = lax.ppermute(texts_out, "inner", beside)
    guests = lax.ppermute(images, "outer", to_previous)
    guests_across = lax.ppermute(images_across, "outer", to_previous)
    texts_beside_core = lax.ppermute(texts_beside, "inner", other_core)
    all_texts = (texts, texts_core, texts_beside, texts_beside_core)

    block = rows * width * 4 * rows * 2
    guests_outs = [((rows, 4 * rows), BF16), ((rows, width), BF16)]
    guests_coef, guests_part = local_call(
        guests_kernel, guests_outs, 2 * block, stretch, offset_term, guests, *all_texts
    )
    back = lax.ppermute(guests_part, "outer", to_next)
    guests_across, guests_part = lax.optimization_barrier((guests_across, guests_part))
    last_coef, last_part = local_call(
        guests_kernel, guests_outs, 2 * block, stretch, offset_term, guests_across, *all_texts
    )
    back_across = lax.ppermute(last_part, "outer", to_next)
    own, own_across, mine, far, for_core = local_call(
        rest_kernel,
        [((rows, width), F32)] * 4 + [((2 * rows, width), BF16)],
        8 * block,
        stretch, offset_term, images, images_across, guests, guests_across,
        guests_coef, last_coef, *all_texts,
    )
    from_core = lax.ppermute(for_core, "inner", other_core)
    back, own_across, back_across = lax.optimization_barrier((back, own_across, back_across))
    mine = mine + from_core[rows:].astype(F32)
    sent = (far + from_core[:rows].astype(F32)).astype(BF16)
    from_beside = lax.ppermute(sent, "inner", beside)
    from_across = lax.ppermute(
        (own_across + back_across.astype(F32)).astype(BF16), "inner", across
    )
    grad_text = mine + from_beside.astype(F32)
    grad_image = own + back.astype(F32) + from_across.astype(F32)
    return grad_image, grad_text


def solution(mesh):
    block = P(("outer", "inner"), None)
    return jax.shard_map(
        per_device,
        mesh=mesh,
        in_specs=(block, block, P(), P()),
        out_specs=(block, block),
        check_vma=False,
    )
```

```python
import jax
import jax.numpy as jnp
from jax import lax
from jax.experimental import pallas as pl
from jax.experimental.pallas import tpu as pltpu
from jax.sharding import PartitionSpec as P

F32 = jnp.float32
BF16 = jnp.bfloat16
BY_COLUMN = (((0,), (0,)), ((), ()))
BY_ROW = (((1,), (1,)), ((), ()))


def inner_route(move, devices):
    route = []
    for chip in range(devices // 2):
        for core in range(2):
            to_chip, to_core = move(chip, core)
            route.append((chip * 2 + core, to_chip * 2 + to_core))
    return route


def stack(*refs):
    return jnp.concatenate([ref[...] for ref in refs], axis=0)


def scores_of(left, right, stretch, offset_term):
    product = lax.dot_general(left, right, BY_ROW, preferred_element_type=F32)
    return stretch[0] * product + offset_term[0]


def guests_kernel(stretch, offset_term, left, t0, t1, t2, t3, coef, part):
    texts = stack(t0, t1, t2, t3)
    scores = scores_of(left[...], texts, stretch, offset_term)
    c = (stretch[0] * jax.nn.sigmoid(scores)).astype(BF16)
    coef[...] = c
    part[...] = jnp.dot(c, texts, preferred_element_type=F32).astype(BF16)


def rest_kernel(
    stretch, offset_term, images, across, guests, last, guests_coef, last_coef, t0, t1, t2, t3,
    own, own_across, mine, far, for_core,
):
    rows = images.shape[0]
    texts = stack(t0, t1, t2, t3)
    scores = scores_of(stack(images, across), texts, stretch, offset_term)
    row = lax.broadcasted_iota(jnp.int32, scores.shape, 0)
    column = lax.broadcasted_iota(jnp.int32, scores.shape, 1)
    same = (row == column) & (row < rows)
    coef = jnp.where(
        same,
        (-stretch[0] * jax.nn.sigmoid(-scores)).astype(BF16),
        (stretch[0] * jax.nn.sigmoid(scores)).astype(BF16),
    )
    image_grads = jnp.dot(coef, texts, preferred_element_type=F32)
    own[...] = image_grads[:rows]
    own_across[...] = image_grads[rows:]
    text_grads = lax.dot_general(
        jnp.concatenate([coef, guests_coef[...], last_coef[...]], axis=0),
        stack(images, across, guests, last),
        BY_COLUMN,
        preferred_element_type=F32,
    )
    mine[...] = text_grads[:rows]
    far[...] = text_grads[2 * rows : 3 * rows]
    for_core[rows:, :] = text_grads[rows : 2 * rows].astype(BF16)
    for_core[:rows, :] = text_grads[3 * rows :].astype(BF16)


def local_call(kernel, outs, flops, stretch, offset_term, *arrays):
    vmem = pl.BlockSpec(memory_space=pltpu.VMEM)
    return pl.pallas_call(
        kernel,
        out_shape=[jax.ShapeDtypeStruct(shape, dtype) for shape, dtype in outs],
        in_specs=[pl.BlockSpec(memory_space=pltpu.SMEM)] * 2 + [vmem] * len(arrays),
        out_specs=[vmem] * len(outs),
        compiler_params=pltpu.CompilerParams(vmem_limit_bytes=24 * 1024 * 1024),
        cost_estimate=pl.CostEstimate(flops=flops, bytes_accessed=0, transcendentals=0),
    )(stretch, offset_term, *arrays)


def per_device(images, texts, stretch, offset_term):
    outer, inner = lax.axis_size("outer"), lax.axis_size("inner")
    chips = inner // 2
    rows, width = images.shape

    across = inner_route(lambda z, c: (chips - 1 - z, c), inner)
    beside = inner_route(lambda z, c: (z ^ 1, c), inner)
    other_core = inner_route(lambda z, c: (z, 1 - c), inner)
    to_previous = [(i, (i - 1) % outer) for i in range(outer)]
    to_next = [(i, (i + 1) % outer) for i in range(outer)]

    images_across = lax.ppermute(images, "inner", across)
    texts_core = lax.ppermute(texts, "inner", other_core)
    texts_beside = lax.ppermute(texts, "inner", beside)
    guests = lax.ppermute(images, "outer", to_previous)
    guests_across = lax.ppermute(images_across, "outer", to_previous)
    texts_beside_core = lax.ppermute(texts_beside, "inner", other_core)
    all_texts = (texts, texts_core, texts_beside, texts_beside_core)

    block = rows * width * 4 * rows * 2
    guests_outs = [((rows, 4 * rows), BF16), ((rows, width), BF16)]
    guests_coef, guests_part = local_call(
        guests_kernel, guests_outs, 2 * block, stretch, offset_term, guests, *all_texts
    )
    back = lax.ppermute(guests_part, "outer", to_next)
    last_coef, last_part = local_call(
        guests_kernel, guests_outs, 2 * block, stretch, offset_term, guests_across, *all_texts
    )
    back_across = lax.ppermute(last_part, "outer", to_next)
    own, own_across, mine, far, for_core = local_call(
        rest_kernel,
        [((rows, width), F32)] * 4 + [((2 * rows, width), BF16)],
        8 * block,
        stretch, offset_term, images, images_across, guests, guests_across,
        guests_coef, last_coef, *all_texts,
    )
    from_core = lax.ppermute(for_core, "inner", other_core)
    own, own_across, back_across = lax.optimization_barrier((own, own_across, back_across))
    mine = mine + from_core[rows:].astype(F32)
    sent = (far + from_core[:rows].astype(F32)).astype(BF16)
    across_sent = (own_across + back_across.astype(F32)).astype(BF16)
    from_beside = lax.ppermute(sent, "inner", beside)
    from_across = lax.ppermute(across_sent, "inner", across)
    grad_text = mine + from_beside.astype(F32)
    grad_image = own + back.astype(F32) + from_across.astype(F32)
    return grad_image, grad_text


def solution(mesh):
    block = P(("outer", "inner"), None)
    return jax.shard_map(
        per_device,
        mesh=mesh,
        in_specs=(block, block, P(), P()),
        out_specs=(block, block),
        check_vma=False,
    )
```

```python
import jax
import jax.numpy as jnp
from jax import lax
from jax.experimental import pallas as pl
from jax.experimental.pallas import tpu as pltpu
from jax.sharding import PartitionSpec as P

F32 = jnp.float32
BF16 = jnp.bfloat16
BY_COLUMN = (((0,), (0,)), ((), ()))
BY_ROW = (((1,), (1,)), ((), ()))


def inner_route(move, devices):
    route = []
    for chip in range(devices // 2):
        for core in range(2):
            to_chip, to_core = move(chip, core)
            route.append((chip * 2 + core, to_chip * 2 + to_core))
    return route


def stack(*refs):
    return jnp.concatenate([ref[...] for ref in refs], axis=0)


def scores_of(left, right, stretch, offset_term):
    product = lax.dot_general(left, right, BY_ROW, preferred_element_type=F32)
    return stretch[0] * product + offset_term[0]


def guests_kernel(stretch, offset_term, left, t0, t1, t2, t3, coef, part):
    texts = stack(t0, t1, t2, t3)
    scores = scores_of(left[...], texts, stretch, offset_term)
    c = (stretch[0] * jax.nn.sigmoid(scores)).astype(BF16)
    coef[...] = c
    part[...] = jnp.dot(c, texts, preferred_element_type=F32).astype(BF16)


def own_kernel(
    stretch, offset_term, images, across, t0, t1, t2, t3, coef_out, own, own_across
):
    rows = images.shape[0]
    texts = stack(t0, t1, t2, t3)
    scores = scores_of(stack(images, across), texts, stretch, offset_term)
    row = lax.broadcasted_iota(jnp.int32, scores.shape, 0)
    column = lax.broadcasted_iota(jnp.int32, scores.shape, 1)
    same = (row == column) & (row < rows)
    coef = jnp.where(
        same,
        (-stretch[0] * jax.nn.sigmoid(-scores)).astype(BF16),
        (stretch[0] * jax.nn.sigmoid(scores)).astype(BF16),
    )
    coef_out[...] = coef
    image_grads = jnp.dot(coef, texts, preferred_element_type=F32)
    own[...] = image_grads[:rows]
    own_across[...] = image_grads[rows:]


def texts_kernel(
    images, across, guests, last, own_coef, guests_coef, last_coef, mine, far, for_core
):
    rows = images.shape[0]
    text_grads = lax.dot_general(
        stack(own_coef, guests_coef, last_coef),
        stack(images, across, guests, last),
        BY_COLUMN,
        preferred_element_type=F32,
    )
    mine[...] = text_grads[:rows]
    far[...] = text_grads[2 * rows : 3 * rows]
    for_core[rows:, :] = text_grads[rows : 2 * rows].astype(BF16)
    for_core[:rows, :] = text_grads[3 * rows :].astype(BF16)


def copy_kernel(given, taken):
    taken[...] = given[...]


def in_vmem(array):
    vmem = pl.BlockSpec(memory_space=pltpu.VMEM)
    return pl.pallas_call(
        copy_kernel,
        out_shape=jax.ShapeDtypeStruct(array.shape, array.dtype),
        in_specs=[vmem],
        out_specs=vmem,
        compiler_params=pltpu.CompilerParams(vmem_limit_bytes=24 * 1024 * 1024),
    )(array)


def local_call(kernel, outs, flops, scalars, *arrays):
    vmem = pl.BlockSpec(memory_space=pltpu.VMEM)
    return pl.pallas_call(
        kernel,
        out_shape=[jax.ShapeDtypeStruct(shape, dtype) for shape, dtype in outs],
        in_specs=[pl.BlockSpec(memory_space=pltpu.SMEM)] * len(scalars) + [vmem] * len(arrays),
        out_specs=[vmem] * len(outs),
        compiler_params=pltpu.CompilerParams(vmem_limit_bytes=24 * 1024 * 1024),
        cost_estimate=pl.CostEstimate(flops=flops, bytes_accessed=0, transcendentals=0),
    )(*scalars, *arrays)


def per_device(images, texts, stretch, offset_term):
    outer, inner = lax.axis_size("outer"), lax.axis_size("inner")
    chips = inner // 2
    rows, width = images.shape

    across = inner_route(lambda z, c: (chips - 1 - z, c), inner)
    beside = inner_route(lambda z, c: (z ^ 1, c), inner)
    other_core = inner_route(lambda z, c: (z, 1 - c), inner)
    to_previous = [(i, (i - 1) % outer) for i in range(outer)]
    to_next = [(i, (i + 1) % outer) for i in range(outer)]

    images_across = lax.ppermute(images, "inner", across)
    texts_core = lax.ppermute(texts, "inner", other_core)
    texts_beside = lax.ppermute(texts, "inner", beside)
    guests = lax.ppermute(images, "outer", to_previous)
    texts_here = in_vmem(texts)
    images_across, texts_here = lax.optimization_barrier((images_across, texts_here))
    guests_across = lax.ppermute(images_across, "outer", to_previous)
    texts_beside_core = lax.ppermute(texts_beside, "inner", other_core)
    all_texts = (texts_here, texts_core, texts_beside, texts_beside_core)

    block = rows * width * 4 * rows * 2
    scalars = (stretch, offset_term)
    guests_outs = [((rows, 4 * rows), BF16), ((rows, width), BF16)]
    last_coef, last_part = local_call(
        guests_kernel, guests_outs, 2 * block, scalars, guests_across, *all_texts
    )
    back_across = lax.ppermute(last_part, "outer", to_next)
    last_coef, images_across = lax.optimization_barrier((last_coef, images_across))
    own_coef, own, own_across = local_call(
        own_kernel,
        [((2 * rows, 4 * rows), BF16)] + [((rows, width), F32)] * 2,
        4 * block,
        scalars, images, images_across, *all_texts,
    )
    guests, own_coef = lax.optimization_barrier((guests, own_coef))
    guests_coef, guests_part = local_call(
        guests_kernel, guests_outs, 2 * block, scalars, guests, *all_texts
    )
    back = lax.ppermute(guests_part, "outer", to_next)
    mine, far, for_core = local_call(
        texts_kernel,
        [((rows, width), F32)] * 2 + [((2 * rows, width), BF16)],
        4 * block,
        (), images, images_across, guests, guests_across, own_coef, guests_coef, last_coef,
    )
    from_core = lax.ppermute(for_core, "inner", other_core)
    own, own_across, back_across = lax.optimization_barrier((own, own_across, back_across))
    mine = mine + from_core[rows:].astype(F32)
    sent = (far + from_core[:rows].astype(F32)).astype(BF16)
    across_sent = (own_across + back_across.astype(F32)).astype(BF16)
    from_beside = lax.ppermute(sent, "inner", beside)
    from_across = lax.ppermute(across_sent, "inner", across)
    grad_text = mine + from_beside.astype(F32)
    grad_image = own + back.astype(F32) + from_across.astype(F32)
    return grad_image, grad_text


def solution(mesh):
    block = P(("outer", "inner"), None)
    return jax.shard_map(
        per_device,
        mesh=mesh,
        in_specs=(block, block, P(), P()),
        out_specs=(block, block),
        check_vma=False,
    )
```

```python
import jax
import jax.numpy as jnp
from jax import lax
from jax.experimental import pallas as pl
from jax.experimental.pallas import tpu as pltpu
from jax.sharding import PartitionSpec as P

F32 = jnp.float32
BF16 = jnp.bfloat16
BY_COLUMN = (((0,), (0,)), ((), ()))
BY_ROW = (((1,), (1,)), ((), ()))


def inner_route(move, devices):
    route = []
    for chip in range(devices // 2):
        for core in range(2):
            to_chip, to_core = move(chip, core)
            route.append((chip * 2 + core, to_chip * 2 + to_core))
    return route


def stack(*refs):
    return jnp.concatenate([ref[...] for ref in refs], axis=0)


def scores_of(left, right, stretch, offset_term):
    product = lax.dot_general(left, right, BY_ROW, preferred_element_type=F32)
    return stretch[0] * product + offset_term[0]


def guests_kernel(stretch, offset_term, left, t0, t1, t2, t3, coef, part):
    texts = stack(t0, t1, t2, t3)
    scores = scores_of(left[...], texts, stretch, offset_term)
    c = (stretch[0] * jax.nn.sigmoid(scores)).astype(BF16)
    coef[...] = c
    part[...] = jnp.dot(c, texts, preferred_element_type=F32).astype(BF16)


def own_kernel(
    stretch, offset_term, images, across, t0, t1, t2, t3, coef_out, own, own_across
):
    rows = images.shape[0]
    texts = stack(t0, t1, t2, t3)
    scores = scores_of(stack(images, across), texts, stretch, offset_term)
    row = lax.broadcasted_iota(jnp.int32, scores.shape, 0)
    column = lax.broadcasted_iota(jnp.int32, scores.shape, 1)
    same = (row == column) & (row < rows)
    coef = jnp.where(
        same,
        (-stretch[0] * jax.nn.sigmoid(-scores)).astype(BF16),
        (stretch[0] * jax.nn.sigmoid(scores)).astype(BF16),
    )
    coef_out[...] = coef
    image_grads = jnp.dot(coef, texts, preferred_element_type=F32)
    own[...] = image_grads[:rows]
    own_across[...] = image_grads[rows:]


def texts_kernel(
    images, across, guests, last, own_coef, guests_coef, last_coef, mine, far, for_core
):
    rows = images.shape[0]
    text_grads = lax.dot_general(
        stack(own_coef, guests_coef, last_coef),
        stack(images, across, guests, last),
        BY_COLUMN,
        preferred_element_type=F32,
    )
    mine[...] = text_grads[:rows]
    far[...] = text_grads[2 * rows : 3 * rows]
    for_core[rows:, :] = text_grads[rows : 2 * rows].astype(BF16)
    for_core[:rows, :] = text_grads[3 * rows :].astype(BF16)


def copy_kernel(stretch, offset_term, given, taken):
    del stretch, offset_term
    taken[...] = given[...]


def in_vmem(stretch, offset_term, array):
    vmem = pl.BlockSpec(memory_space=pltpu.VMEM)
    return pl.pallas_call(
        copy_kernel,
        out_shape=jax.ShapeDtypeStruct(array.shape, array.dtype),
        in_specs=[pl.BlockSpec(memory_space=pltpu.SMEM)] * 2 + [vmem],
        out_specs=vmem,
        compiler_params=pltpu.CompilerParams(vmem_limit_bytes=24 * 1024 * 1024),
    )(stretch, offset_term, array)


def local_call(kernel, outs, flops, scalars, *arrays):
    vmem = pl.BlockSpec(memory_space=pltpu.VMEM)
    return pl.pallas_call(
        kernel,
        out_shape=[jax.ShapeDtypeStruct(shape, dtype) for shape, dtype in outs],
        in_specs=[pl.BlockSpec(memory_space=pltpu.SMEM)] * len(scalars) + [vmem] * len(arrays),
        out_specs=[vmem] * len(outs),
        compiler_params=pltpu.CompilerParams(vmem_limit_bytes=24 * 1024 * 1024),
        cost_estimate=pl.CostEstimate(flops=flops, bytes_accessed=0, transcendentals=0),
    )(*scalars, *arrays)


def per_device(images, texts, stretch, offset_term):
    outer, inner = lax.axis_size("outer"), lax.axis_size("inner")
    chips = inner // 2
    rows, width = images.shape

    across = inner_route(lambda z, c: (chips - 1 - z, c), inner)
    beside = inner_route(lambda z, c: (z ^ 1, c), inner)
    other_core = inner_route(lambda z, c: (z, 1 - c), inner)
    to_previous = [(i, (i - 1) % outer) for i in range(outer)]
    to_next = [(i, (i + 1) % outer) for i in range(outer)]

    images_across = lax.ppermute(images, "inner", across)
    texts_core = lax.ppermute(texts, "inner", other_core)
    texts_beside = lax.ppermute(texts, "inner", beside)
    guests = lax.ppermute(images, "outer", to_previous)
    texts_here = in_vmem(stretch, offset_term, texts)
    images_across, texts_here = lax.optimization_barrier((images_across, texts_here))
    guests_across = lax.ppermute(images_across, "outer", to_previous)
    texts_beside_core = lax.ppermute(texts_beside, "inner", other_core)
    all_texts = (texts_here, texts_core, texts_beside, texts_beside_core)

    block = rows * width * 4 * rows * 2
    scalars = (stretch, offset_term)
    guests_outs = [((rows, 4 * rows), BF16), ((rows, width), BF16)]
    last_coef, last_part = local_call(
        guests_kernel, guests_outs, 2 * block, scalars, guests_across, *all_texts
    )
    back_across = lax.ppermute(last_part, "outer", to_next)
    last_coef, images_across = lax.optimization_barrier((last_coef, images_across))
    own_coef, own, own_across = local_call(
        own_kernel,
        [((2 * rows, 4 * rows), BF16)] + [((rows, width), F32)] * 2,
        4 * block,
        scalars, images, images_across, *all_texts,
    )
    guests, own_coef = lax.optimization_barrier((guests, own_coef))
    guests_coef, guests_part = local_call(
        guests_kernel, guests_outs, 2 * block, scalars, guests, *all_texts
    )
    back = lax.ppermute(guests_part, "outer", to_next)
    mine, far, for_core = local_call(
        texts_kernel,
        [((rows, width), F32)] * 2 + [((2 * rows, width), BF16)],
        4 * block,
        (), images, images_across, guests, guests_across, own_coef, guests_coef, last_coef,
    )
    from_core = lax.ppermute(for_core, "inner", other_core)
    own, own_across, back_across = lax.optimization_barrier((own, own_across, back_across))
    mine = mine + from_core[rows:].astype(F32)
    sent = (far + from_core[:rows].astype(F32)).astype(BF16)
    across_sent = (own_across + back_across.astype(F32)).astype(BF16)
    from_beside = lax.ppermute(sent, "inner", beside)
    from_across = lax.ppermute(across_sent, "inner", across)
    grad_text = mine + from_beside.astype(F32)
    grad_image = own + back.astype(F32) + from_across.astype(F32)
    return grad_image, grad_text


def solution(mesh):
    block = P(("outer", "inner"), None)
    return jax.shard_map(
        per_device,
        mesh=mesh,
        in_specs=(block, block, P(), P()),
        out_specs=(block, block),
        check_vma=False,
    )
```
